32 devices in a mesh: grp: 2 (over y), tm: 4 (over z), space: 4 (over x, core).
Axes of the slice: x: 2, y: 2, z: 4, core: 2. Of those that a mesh axis runs over, the one named last changes fastest.
Arguments:
- solutions: bfloat16 [128, 4, 2, 3, 256, 128], P(('grp', 'tm'), None, None, None, 'space'), parts along dimension 0, may hold values from -6 to 6
- eigvecs: bfloat16 [4, 2, 3, 256, 128], P('tm', None, None, 'space'), may hold values from -0.15625 to 0.15625
- sink_time: int32 [128, 1], P(('grp', 'tm')), parts along dimension 0, may hold values from 0 to 3; in each aligned block of 16 rows (0 to 15, 16 to 31, ...) at most 8 rows name the same one
Outputs:
- perambulator: bfloat16 [128, 4, 2, 128, 128], P(('grp', 'tm'), None, None, 'space'), parts along dimension 0
The draws below stay inside these ranges and needn't reach their ends.
There are 2 independent parts, one for each index of `grp`. The reference program is written for one: setup_inputs(seed, part) draws one part's arguments, and reference() takes and returns one part's arrays. A program takes and returns all parts, laid end to end along the dimension named above; an argument that names none is the same for every part. Nothing has to cross between parts.
Inputs may be any that keep to these rules, and one draw needn't show every extreme that they name: `sink_time`: among the rows of one device (aligned blocks of 16 rows) no timeslice is named by more than 8 rows, a bound that some block reaches of them.
All inputs are finite; a program needn't handle non-finite values.
Results may differ from the reference program's by a relative error of at most 0.012.
Values may be sent and summed in bfloat16 or wider, within the bound.
No kernel may reach another device: no remote copies, remote signals or barrier semaphores. Data moves between devices by JAX's collectives and lax.ppermute only.
A program may use at most 128 MiB of HBM per device.

```python
import math
import jax
import jax.numpy as jnp
import numpy as np
from jax import lax

E = 128
COLS = 128
NSPIN = 4
NCOL = 3
XS = 64
BLK = 16
CAP = 8
NT = 4
SITES = 256
BLOCKS = 64
N_SPACE = 4


def steps_of(key, shape, pieces, smallest, high):
    factor_of = 1.0
    for axis_at, shards_of in pieces:
        draws = jax.random.uniform(jax.random.fold_in(jax.random.fold_in(key, 6), axis_at), (shards_of,), jnp.float32, smallest / len(pieces), high / len(pieces))
        factor_of = factor_of * jnp.repeat(jnp.exp(draws), shape[axis_at] // shards_of).reshape((-1,) + (1,) * (len(shape) - 1 - axis_at))
    return factor_of


def shared_out(key, own, number, rows, number_of, top, bound, lean):
    ranking = jax.random.permutation(key, number_of)
    packed, common = portions_of(number_of, rows * top, bound, lean, True), portions_of(number_of, rows * top, bound, lean, False)
    places = jnp.arange(number_of)

    def named(tallies, offset_by):
        used = int((tallies > 0).sum())
        fixed = max(1, used // 4)
        shifted = fixed + (places - fixed + offset_by * (used - fixed)) % max(1, number_of - fixed)
        return jnp.zeros((number_of,), jnp.int32).at[ranking[jnp.where(places < fixed, places, shifted)]].set(jnp.asarray(tallies, jnp.int32))

    tallies = jnp.where(number % 4 == 0, named(packed, number // 4), named(common, number - number // 4 - 1))
    mixed = jax.random.permutation(jax.random.fold_in(own, 3), number_of)
    donor, sink = mixed[0:number_of // 2 * 2:2], mixed[1:number_of // 2 * 2:2]
    room = jnp.minimum(tallies[donor] - 1, bound - tallies[sink]) // 2
    room = jnp.where((donor == ranking[0]) | (sink == ranking[0]) | (tallies[sink] == 0), 0, jnp.maximum(room, 0))
    shifted = jax.random.randint(jax.random.fold_in(own, 4), (number_of // 2,), 0, 1 << 20) % (room + 1)
    tallies = tallies.at[donor].add(-shifted).at[sink].add(shifted)
    members = jnp.searchsorted(jnp.cumsum(tallies), jnp.arange(rows * top), side="right").astype(jnp.int32)
    listing = members.reshape(top, rows).T
    listing = listing[jax.random.permutation(jax.random.fold_in(own, 1), rows)]
    offset_by = jax.random.randint(jax.random.fold_in(own, 2), (rows, 1), 0, top)
    return jnp.take_along_axis(listing, (jnp.arange(top)[None, :] + offset_by) % top, axis=1)


def portions_of(amount, total, most, slope, full):
    portions = [(1 << 20) // math.isqrt(standing ** slope) + 1 for standing in range(1, amount + 1)]
    largest = most if full else min(most, max(-(-total // amount), total * portions[0] // sum(portions)))
    least = 1 if total - largest >= amount - 1 else 0
    given, rest = [largest] + [least] * (amount - 1), total - largest - least * (amount - 1)
    while rest > 0:
        candidates = [i for i in range(1, amount) if given[i] < largest] or [i for i in range(1, amount) if given[i] < most]
        pool, left = sum([portions[i] for i in candidates]), rest
        for i in candidates:
            extra = min(most - given[i], max(1, left * portions[i] // pool), rest)
            given[i] = given[i] + extra
            rest = rest - extra
    return np.array(given)


def normal_values(stream_key, extent, deviation, reach, split=(), kind=jnp.bfloat16):
    array = deviation * jax.random.normal(stream_key, extent, jnp.float32)
    if split:
        array = array * steps_of(stream_key, extent, split, -0.22, 0.18)
    return jnp.clip(array, -reach, reach).astype(kind)


def setup_inputs(seed: int = 0, part: int = 0) -> dict:
    splits = jax.random.split(jax.random.key(seed), 4)
    part_splits = jax.random.split(jax.random.fold_in(splits[3], part), 4)
    solutions = normal_values(part_splits[0], (BLOCKS, NSPIN, 2, NCOL, SITES, COLS), 1.0, 6.0, ((0, 4), (4, 4)))
    eigvecs = normal_values(splits[1], (NT, 2, NCOL, SITES, E), (2 * NCOL * SITES) ** -0.5, 0.15625, ((0, 4), (3, 4)))
    sink_time_keys = jax.random.split(jax.random.fold_in(part_splits[2], 1), BLOCKS // BLK)
    sink_time_turns = jax.random.permutation(jax.random.fold_in(part_splits[2], 3), BLOCKS // BLK)
    sink_time = jax.vmap(lambda own, number: shared_out(jax.random.fold_in(part_splits[2], 2), own, number, BLK, NT, 1, CAP, 2))(sink_time_keys, sink_time_turns).reshape((BLOCKS, 1))
    return {"solutions": solutions, "eigvecs": eigvecs, "sink_time": sink_time}


def reference(solutions, eigvecs, sink_time):
    def project_block(pair):
        block_data, timeslice = pair
        vector = lax.dynamic_index_in_dim(eigvecs, timeslice, 0, keepdims=False)
        left_matrix = jnp.stack([vector, jnp.stack([-vector[1], vector[0]])])
        left_matrix = left_matrix.reshape(2, 2, NCOL, N_SPACE, XS, E).astype(jnp.float32)
        right_matrix = block_data.reshape(NSPIN, 2, NCOL, N_SPACE, XS, COLS).astype(jnp.float32)
        partial_terms = jnp.einsum("orcgxe,srcgxj->gsoej", left_matrix, right_matrix)
        partial_terms = partial_terms.astype(jnp.bfloat16).astype(jnp.float32)
        return jnp.sum(partial_terms, axis=0).astype(jnp.bfloat16)

    return lax.map(project_block, (solutions, sink_time[:, 0].astype(jnp.int32)))
```

```python
import functools

import jax
import jax.numpy as jnp
from jax import lax
from jax.experimental import pallas as pl
from jax.experimental.pallas import tpu as pltpu
from jax.sharding import PartitionSpec as P

SMEM = pl.BlockSpec(memory_space=pltpu.SMEM)
VMEM = pl.BlockSpec(memory_space=pltpu.VMEM)
ANY = pl.BlockSpec(memory_space=pl.ANY)
HBM = pl.BlockSpec(memory_space=pltpu.HBM)
LITTLE = pl.CostEstimate(flops=1, bytes_accessed=1, transcendentals=0)
MUCH = pl.CostEstimate(flops=20_000_000_000, bytes_accessed=80_000_000, transcendentals=0)
PARAMS = pltpu.CompilerParams(vmem_limit_bytes=16 * 1024 * 1024)


def near(array):
    return pltpu.with_memory_space_constraint(array, pltpu.VMEM)


def far(array):
    return pltpu.with_memory_space_constraint(array, pltpu.HBM)


def in_pairs(count):
    return count & (count - 1) == 0


def peer(index, step, count):
    return index ^ step if in_pairs(count) else (index + step) % count


def apart(here, there, count):
    return here ^ there if in_pairs(count) else lax.rem(there - here + count, count)


def swap(array, axis, step, count):
    return lax.ppermute(array, axis, [(i, peer(i, step, count)) for i in range(count)])


def call(kernel, ins, outs, operands, cost=LITTLE, **more):
    specs, shapes = zip(*outs)
    return pl.pallas_call(
        kernel,
        in_specs=ins,
        out_specs=specs,
        out_shape=shapes,
        cost_estimate=cost,
        compiler_params=PARAMS,
        **more,
    )(*operands)


def load(steps, first, times_ref, place_ref, data_ref, order_ref, slot_ref, held_ref, sem):
    blocks = times_ref.shape[0]
    count = len(steps)
    here = place_ref[0]

    def slot_of(i):
        step = apart(times_ref[i], here, count)
        slot = jnp.int32(0)
        for at, value in enumerate(steps):
            slot = jnp.where(step == value, at, slot)
        return slot

    def count_early(i, total):
        return total + (slot_of(i) < first).astype(jnp.int32)

    early = lax.fori_loop(0, blocks, count_early, jnp.int32(0))

    def copy(block, where):
        return pltpu.make_async_copy(data_ref.at[block], held_ref.at[where], sem.at[where])

    def place(i, at):
        low, high = at
        slot = slot_of(i)
        is_early = slot < first
        where = jnp.where(is_early, low, high)
        order_ref[where] = i
        slot_ref[where] = slot
        copy(i, where).start()
        one = is_early.astype(jnp.int32)
        return low + one, high + 1 - one

    lax.fori_loop(0, blocks, place, (jnp.int32(0), early))
    for where in range(blocks):
        copy(order_ref[where], where).wait()


def join(*refs):
    for at, ref in enumerate(refs[:-1]):
        refs[-1][at] = ref[...]


def project_sites(chips, width, size, vectors, place_ref, slot_ref, *refs):
    vector_refs, held_ref = refs[:vectors], refs[vectors]
    outs, left_ref = refs[vectors + 1 : -1], refs[-1]
    spins, columns = held_ref.shape[1], held_ref.shape[-1]
    rows = 2 * width
    chip, core = place_ref[1], place_ref[2]
    for slot, ref in enumerate(vector_refs):
        real, imag = ref[0], ref[1]
        for part, pair in enumerate(((real, imag), (-imag, real))):
            turned = jnp.concatenate(pair, axis=0).T
            for to_chip in range(chips):
                for to_core in range(2):
                    stays = (core == to_core).astype(jnp.int32)
                    at = ((stays * chips + apart(chip, to_chip, chips)) * 2 + part) * width
                    start = (to_chip * 2 + to_core) * width
                    left_ref[slot, pl.ds(pl.multiple_of(at, width), width), :] = turned[
                        start : start + width
                    ]
    for piece in range(len(outs) // 2):
        give_ref, keep_ref = outs[2 * piece : 2 * piece + 2]
        for i in range(size):
            left = left_ref[slot_ref[piece * size + i]]
            for spin in range(0, spins, 2):
                right = jnp.concatenate(
                    [
                        held_ref[piece * size + i, s].reshape(-1, columns)
                        for s in range(spin, spin + 2)
                    ],
                    axis=1,
                )
                result = jnp.dot(left, right, preferred_element_type=jnp.float32)
                result = result.astype(give_ref.dtype)
                for s in range(2):
                    side = result[:, s * columns : (s + 1) * columns]
                    for ref, part in ((give_ref, side[: chips * rows]), (keep_ref, side[chips * rows :])):
                        ref[:, i, spin + s] = part.reshape(chips, rows, columns)


def project_chip(chips, width, start, size, vectors, place_ref, order_ref, slot_ref, *refs):
    if vectors:
        vector_refs, others_ref = refs[:vectors], refs[vectors]
        held_ref, other_ref = refs[vectors + 1 : vectors + 3]
        outs = refs[vectors + 3 : -2]
        left_ref = outs[chips]
    else:
        left_ref, held_ref, other_ref = refs[:3]
        outs = refs[3:-2]
    came_ref, sem = refs[-2:]
    spins, columns = held_ref.shape[1], held_ref.shape[-1]
    rows = 2 * width

    def copy(i):
        return pltpu.make_async_copy(
            other_ref.at[order_ref[start + i]], came_ref.at[i], sem.at[i]
        )

    for i in range(size):
        copy(i).start()
    chip, core = place_ref[1], place_ref[2]
    for slot in range(vectors):
        real, imag = (
            jnp.concatenate([vector_refs[slot][part], others_ref[slot, part]], axis=0)
            for part in range(2)
        )
        for part, pair in enumerate(((real, imag), (-imag, real))):
            turned = jnp.concatenate(pair, axis=0).T
            for to_chip in range(chips):
                at = (apart(chip, to_chip, chips) * 2 + part) * width
                low = to_chip * 2 * width
                left_ref[slot, pl.ds(pl.multiple_of(at, width), width), :] = jnp.where(
                    core == 0,
                    turned[low : low + width],
                    turned[low + width : low + 2 * width],
                )
    for i in range(size):
        left = left_ref[slot_ref[start + i]]
        copy(i).wait()
        for spin in range(0, spins, 2):
            right = jnp.concatenate(
                [
                    jnp.concatenate(
                        [
                            ref[at, s, part]
                            for part in range(2)
                            for ref, at in ((held_ref, start + i), (came_ref, i))
                        ],
                        axis=0,
                    )
                    for s in range(spin, spin + 2)
                ],
                axis=1,
            )
            result = jnp.dot(left, right, preferred_element_type=jnp.float32)
            result = result.astype(outs[0].dtype)
            for s in range(2):
                for step in range(chips):
                    outs[step][i, spin + s] = result[
                        step * rows : (step + 1) * rows, s * columns : (s + 1) * columns
                    ]


def finish(start, size, terms, order_ref, *refs):
    out_ref, stage_ref, sem = refs[-3:]

    def copy(i):
        return pltpu.make_async_copy(stage_ref.at[i], out_ref.at[order_ref[start + i]], sem.at[i])

    for i in range(size):
        total = None
        for ref in refs[:terms]:
            term = ref[i] if len(ref.shape) == 4 else ref[0, i]
            term = term.astype(jnp.float32)
            total = term if total is None else total + term
        stage_ref[i] = total.reshape(stage_ref.shape[1:]).astype(stage_ref.dtype)
        copy(i).start()
    for i in range(size):
        copy(i).wait()


def shards(solutions, eigvecs, sink_time):
    blocks, spins, _, colours, sites, columns = solutions.shape
    times = lax.axis_size("tm")
    members = lax.axis_size("space")
    chips = members // 2
    width = eigvecs.shape[-1] // members
    rows = 2 * width
    depth = 2 * colours * sites
    kind = solutions.dtype
    at = lax.axis_index("space")
    place = jnp.stack([lax.axis_index("tm"), at // 2, at % 2]).astype(jnp.int32)
    cores = [(i, i ^ 1) for i in range(members)]

    most = max(2, (2 * blocks + times - 1) // times)
    half = blocks // 2
    late = half // most
    first = times - late
    steps = [0] + list(range(1, times, 2)) + list(range(2, times, 2))

    own = eigvecs[0].reshape(2, colours * sites, -1)
    data = solutions.reshape(blocks, spins, 2, colours * sites, columns)
    other_data = lax.ppermute(data, "space", cores)
    vectors = [own]
    for slot, step in enumerate(steps[1:], 1):
        if slot >= first and in_pairs(times) and steps.index(step ^ 1) < first:
            vectors.append(swap(vectors[steps.index(step ^ 1)], "tm", 1, times))
        else:
            vectors.append(swap(own, "tm", step, times))

    numbers = jax.ShapeDtypeStruct((blocks,), jnp.int32)
    order, slots, held = call(
        functools.partial(load, steps, first),
        [SMEM, SMEM, HBM],
        [(SMEM, numbers), (SMEM, numbers), (VMEM, pltpu.VMEM(data.shape, kind))],
        [sink_time[:, 0], place, far(data)],
        scratch_shapes=[pltpu.SemaphoreType.DMA((blocks,))],
    )
    held = near(held)

    size = half // 2
    piece = pltpu.VMEM((chips, size, spins, rows, columns), kind)
    pieces = call(
        functools.partial(project_sites, chips, width, size, first),
        [SMEM, SMEM] + [VMEM] * (first + 1),
        [(VMEM, piece)] * 4,
        [place, slots, *[near(v) for v in vectors[:first]], held],
        scratch_shapes=[pltpu.VMEM((first, 4 * chips * width, depth), kind)],
    )
    terms = []
    for give, keep in (pieces[:2], pieces[2:]):
        got = lax.ppermute(give, "space", cores)
        sums = [keep, got]
        for step in range(1, chips):
            sent = (keep[step].astype(jnp.float32) + got[step].astype(jnp.float32)).astype(kind)
            sums.append(send(sent, step, members))
        terms.append(sums)

    vectors = [near(v) for v in vectors]
    (joined,) = call(
        join, [VMEM] * times, [(VMEM, pltpu.VMEM((times, *own.shape), kind))], vectors
    )
    others = near(lax.ppermute(joined, "space", cores))

    piece = pltpu.VMEM((size, spins, rows, columns), kind)
    lefts = (VMEM, pltpu.VMEM((times, chips * rows, 2 * depth), kind))
    left = None
    for start in (half, half + size):
        results = call(
            functools.partial(
                project_chip, chips, width, start, size, times if left is None else 0
            ),
            [SMEM] * 3 + [VMEM] * (times + 2 if left is None else 2) + [HBM],
            [(VMEM, piece)] * chips + ([lefts] if left is None else []),
            [place, order, slots, *([*vectors, others] if left is None else [left]), held, far(other_data)],
            scratch_shapes=[
                pltpu.VMEM((size, *data.shape[1:]), kind),
                pltpu.SemaphoreType.DMA((size,)),
            ],
        )
        if left is None:
            left = near(results[chips])
        terms.append(
            [results[0]] + [send(results[step], step, members) for step in range(1, chips)]
        )

    result = None
    for at, sums in enumerate(terms):
        operands = [order, *[near(a) for a in sums]]
        ins = [SMEM] + [VMEM] * len(sums)
        aliases = {}
        if result is not None:
            aliases = {len(operands): 0}
            operands.append(result)
            ins.append(HBM)
        (result,) = call(
            functools.partial(finish, at * size, size, len(sums)),
            ins,
            [(HBM, jax.ShapeDtypeStruct((blocks, spins, 2, width, columns), kind))],
            operands,
            MUCH,
            scratch_shapes=[
                pltpu.VMEM((size, spins, 2, width, columns), kind),
                pltpu.SemaphoreType.DMA((size,)),
            ],
            input_output_aliases=aliases,
        )
    return result


def send(array, step, members):
    route = [(i, peer(i // 2, step, members // 2) * 2 + i % 2) for i in range(members)]
    return lax.ppermute(array, "space", route)


def solution(mesh):
    in_specs = (
        P(("grp", "tm"), None, None, None, "space", None),
        P("tm", None, None, "space", None),
        P(("grp", "tm"), None),
    )
    out_specs = P(("grp", "tm"), None, None, "space", None)
    return jax.shard_map(shards, mesh=mesh, in_specs=in_specs, out_specs=out_specs, check_vma=False)
```

```python
import functools

import jax
import jax.numpy as jnp
from jax import lax
from jax.experimental import pallas as pl
from jax.experimental.pallas import tpu as pltpu
from jax.sharding import PartitionSpec as P

SHARES = (4, 4, 4, 4)
AFTER = (None, None, 1, 2)
SMEM = pl.BlockSpec(memory_space=pltpu.SMEM)
VMEM = pl.BlockSpec(memory_space=pltpu.VMEM)
ANY = pl.BlockSpec(memory_space=pl.ANY)
HBM = pl.BlockSpec(memory_space=pltpu.HBM)
LITTLE = pl.CostEstimate(flops=1, bytes_accessed=1, transcendentals=0)
COSTS = [LITTLE] * 4
MUCH = pl.CostEstimate(flops=20_000_000_000, bytes_accessed=1, transcendentals=0)
PARAMS = pltpu.CompilerParams(vmem_limit_bytes=16 * 1024 * 1024)


def scalars(array):
    return pltpu.with_memory_space_constraint(array, pltpu.SMEM)


def near(array):
    return pltpu.with_memory_space_constraint(array, pltpu.VMEM)


def far(array):
    return pltpu.with_memory_space_constraint(array, pltpu.HBM)


def in_pairs(count):
    return count & (count - 1) == 0


def peer(index, step, count):
    return index ^ step if in_pairs(count) else (index + step) % count


def apart(here, there, count):
    return here ^ there if in_pairs(count) else lax.rem(there - here + count, count)


def swap(array, axis, step, count):
    return lax.ppermute(array, axis, [(i, peer(i, step, count)) for i in range(count)])


def call(kernel, ins, outs, operands, cost=LITTLE, **more):
    specs, shapes = zip(*outs)
    return pl.pallas_call(
        kernel,
        in_specs=ins,
        out_specs=specs,
        out_shape=shapes,
        cost_estimate=cost,
        compiler_params=PARAMS,
        **more,
    )(*operands)


def load(steps, first, times_ref, place_ref, data_ref, order_ref, slot_ref, spot_ref, held_ref, sem):
    blocks = times_ref.shape[0]
    count = len(steps)
    here = place_ref[0]

    def slot_of(i):
        step = apart(times_ref[i], here, count)
        slot = jnp.int32(0)
        for at, value in enumerate(steps):
            slot = jnp.where(step == value, at, slot)
        return slot

    def count_early(i, total):
        return total + (slot_of(i) < first).astype(jnp.int32)

    early = lax.fori_loop(0, blocks, count_early, jnp.int32(0))

    def copy(block, where):
        return pltpu.make_async_copy(data_ref.at[block], held_ref.at[where], sem.at[where])

    def place(i, at):
        low, high = at
        slot = slot_of(i)
        is_early = slot < first
        where = jnp.where(is_early, low, high)
        order_ref[where] = i
        slot_ref[where] = slot
        copy(i, where).start()
        one = is_early.astype(jnp.int32)
        return low + one, high + 1 - one

    lax.fori_loop(0, blocks, place, (jnp.int32(0), early))
    for i in range(3):
        spot_ref[i] = place_ref[i]
    for where in range(blocks):
        copy(order_ref[where], where).wait()


def turn_sites(chips, width, slot, vector_ref, place_ref, left_ref):
    chip, core = place_ref[1], place_ref[2]
    real, imag = vector_ref[0], vector_ref[1]
    for part, pair in enumerate(((real, imag), (-imag, real))):
        turned = jnp.concatenate(pair, axis=0).T
        for to_chip in range(chips):
            for to_core in range(2):
                stays = (core == to_core).astype(jnp.int32)
                at = ((stays * chips + apart(chip, to_chip, chips)) * 2 + part) * width
                start = (to_chip * 2 + to_core) * width
                left_ref[slot, pl.ds(pl.multiple_of(at, width), width), :] = turned[
                    start : start + width
                ]


def project_sites(chips, width, start, slot_ref, left_ref, held_ref, give_ref, keep_ref):
    spins, columns = held_ref.shape[1], held_ref.shape[-1]
    rows = 2 * width
    for i in range(give_ref.shape[1]):
        left = left_ref[slot_ref[start + i]]
        for spin in range(0, spins, 2):
            right = jnp.concatenate(
                [held_ref[start + i, s].reshape(-1, columns) for s in range(spin, spin + 2)],
                axis=1,
            )
            result = jnp.dot(left, right, preferred_element_type=jnp.float32)
            result = result.astype(give_ref.dtype)
            for s in range(2):
                side = result[:, s * columns : (s + 1) * columns]
                for ref, part in ((give_ref, side[: chips * rows]), (keep_ref, side[chips * rows :])):
                    ref[:, i, spin + s] = part.reshape(chips, rows, columns)


def project(chips, width, start, known, fresh, place_ref, slot_ref, *refs):
    vector_refs, held_ref = refs[:fresh], refs[fresh]
    if fresh:
        give_ref, keep_ref, left_ref = refs[-3:]
        for at, ref in enumerate(vector_refs):
            turn_sites(chips, width, known + at, ref, place_ref, left_ref)
    else:
        left_ref = refs[1]
        give_ref, keep_ref = refs[-2:]
    project_sites(chips, width, start, slot_ref, left_ref, held_ref, give_ref, keep_ref)


def finish(start, size, terms, order_ref, *refs):
    out_ref, stage_ref, sem = refs[-3:]

    def copy(i):
        return pltpu.make_async_copy(stage_ref.at[i], out_ref.at[order_ref[start + i]], sem.at[i])

    for i in range(size):
        total = None
        for ref in refs[:terms]:
            term = ref[i] if len(ref.shape) == 4 else ref[0, i]
            term = term.astype(jnp.float32)
            total = term if total is None else total + term
        stage_ref[i] = total.reshape(stage_ref.shape[1:]).astype(stage_ref.dtype)
        copy(i).start()
    for i in range(size):
        copy(i).wait()


def shards(solutions, eigvecs, sink_time):
    blocks, spins, _, colours, sites, columns = solutions.shape
    times = lax.axis_size("tm")
    members = lax.axis_size("space")
    chips = members // 2
    width = eigvecs.shape[-1] // members
    rows = 2 * width
    depth = 2 * colours * sites
    kind = solutions.dtype
    at = lax.axis_index("space")
    place = jnp.stack([lax.axis_index("tm"), at // 2, at % 2]).astype(jnp.int32)
    cores = [(i, i ^ 1) for i in range(members)]

    most = max(2, (2 * blocks + times - 1) // times)
    half = blocks // 2
    late = half // most
    first = times - late
    steps = [0] + list(range(1, times, 2)) + list(range(2, times, 2))

    own = eigvecs[0].reshape(2, colours * sites, -1)
    data = solutions.reshape(blocks, spins, 2, colours * sites, columns)
    vectors = [own]
    for slot, step in enumerate(steps[1:], 1):
        if slot >= first and in_pairs(times) and steps.index(step ^ 1) < first:
            vectors.append(swap(vectors[steps.index(step ^ 1)], "tm", 1, times))
        else:
            vectors.append(swap(own, "tm", step, times))

    numbers = pltpu.SMEM((blocks,), jnp.int32)
    order, slots, spot, held = call(
        functools.partial(load, steps, first),
        [SMEM, SMEM, HBM],
        [(SMEM, numbers), (SMEM, numbers), (SMEM, pltpu.SMEM((3,), jnp.int32)), (VMEM, pltpu.VMEM(data.shape, kind))],
        [sink_time[:, 0], place, far(data)],
        scratch_shapes=[pltpu.SemaphoreType.DMA((blocks,))],
    )
    held = near(held)
    order, slots, place = scalars(order), scalars(slots), scalars(spot)

    sizes = [share * blocks // 16 for share in SHARES]
    vectors = [near(v) for v in vectors]
    lefts = (VMEM, pltpu.VMEM((times, 4 * chips * width, depth), kind))
    left = None
    known = start = 0
    terms = []
    sents = []
    for at, size in enumerate(sizes):
        piece = (VMEM, pltpu.VMEM((chips, size, spins, rows, columns), kind))
        wanted = first if start + size <= half else times
        fresh = wanted - known
        after = sents[AFTER[at] : AFTER[at] + 1] if AFTER[at] is not None else []
        operands = [place, slots, *vectors[known:wanted], held]
        ins = [SMEM] * 2 + [VMEM] * (fresh + 1)
        if left is not None:
            operands.append(near(left))
            ins.append(VMEM)
        results = call(
            functools.partial(project, chips, width, start, known, fresh),
            ins + [ANY] * len(after),
            [piece, piece] + [lefts] * bool(fresh),
            operands + after,
            COSTS[at],
            input_output_aliases={len(operands) - 1: 2} if fresh and left is not None else {},
        )
        give, keep = results[:2]
        if fresh:
            left = results[2]
        got = lax.ppermute(give, "space", cores)
        sums = [keep, got]
        for step in range(1, chips):
            sent = (keep[step].astype(jnp.float32) + got[step].astype(jnp.float32)).astype(kind)
            sums.append(send(sent, step, members))
        sents.append(sent)
        terms.append(sums)
        known = wanted
        start += size

    result = None
    start = 0
    for size, sums in zip(sizes, terms):
        operands = [order, *[near(a) for a in sums]]
        ins = [SMEM] + [VMEM] * len(sums)
        aliases = {}
        if result is not None:
            aliases = {len(operands): 0}
            operands.append(result)
            ins.append(HBM)
        (result,) = call(
            functools.partial(finish, start, size, len(sums)),
            ins,
            [(HBM, jax.ShapeDtypeStruct((blocks, spins, 2, width, columns), kind))],
            operands,
            MUCH,
            scratch_shapes=[
                pltpu.VMEM((size, spins, 2, width, columns), kind),
                pltpu.SemaphoreType.DMA((size,)),
            ],
            input_output_aliases=aliases,
        )
        start += size
    return result


def send(array, step, members):
    route = [(i, peer(i // 2, step, members // 2) * 2 + i % 2) for i in range(members)]
    return lax.ppermute(array, "space", route)


def solution(mesh):
    in_specs = (
        P(("grp", "tm"), None, None, None, "space", None),
        P("tm", None, None, "space", None),
        P(("grp", "tm"), None),
    )
    out_specs = P(("grp", "tm"), None, None, "space", None)
    return jax.shard_map(shards, mesh=mesh, in_specs=in_specs, out_specs=out_specs, check_vma=False)
```

```python
import functools

import jax
import jax.numpy as jnp
from jax import lax
from jax.experimental import pallas as pl
from jax.experimental.pallas import tpu as pltpu
from jax.sharding import PartitionSpec as P

SHARES = (4, 4, 8)
AFTER = (None, None, 1)
SMEM = pl.BlockSpec(memory_space=pltpu.SMEM)
VMEM = pl.BlockSpec(memory_space=pltpu.VMEM)
ANY = pl.BlockSpec(memory_space=pl.ANY)
HBM = pl.BlockSpec(memory_space=pltpu.HBM)
LITTLE = pl.CostEstimate(flops=1, bytes_accessed=1, transcendentals=0)
MUCH = pl.CostEstimate(flops=20_000_000_000, bytes_accessed=1, transcendentals=0)
PARAMS = pltpu.CompilerParams(vmem_limit_bytes=16 * 1024 * 1024)


def scalars(array):
    return pltpu.with_memory_space_constraint(array, pltpu.SMEM)


def near(array):
    return pltpu.with_memory_space_constraint(array, pltpu.VMEM)


def far(array):
    return pltpu.with_memory_space_constraint(array, pltpu.HBM)


def in_pairs(count):
    return count & (count - 1) == 0


def peer(index, step, count):
    return index ^ step if in_pairs(count) else (index + step) % count


def apart(here, there, count):
    return here ^ there if in_pairs(count) else lax.rem(there - here + count, count)


def swap(array, axis, step, count):
    return lax.ppermute(array, axis, [(i, peer(i, step, count)) for i in range(count)])


def call(kernel, ins, outs, operands, cost=LITTLE, **more):
    specs, shapes = zip(*outs)
    return pl.pallas_call(
        kernel,
        in_specs=ins,
        out_specs=specs,
        out_shape=shapes,
        cost_estimate=cost,
        compiler_params=PARAMS,
        **more,
    )(*operands)


def load(steps, first, times_ref, data_ref, order_ref, slot_ref, held_ref, sem):
    blocks = times_ref.shape[0]
    count = len(steps)
    here = lax.axis_index("tm")

    def slot_of(i):
        step = apart(times_ref[i], here, count)
        slot = jnp.int32(0)
        for at, value in enumerate(steps):
            slot = jnp.where(step == value, at, slot)
        return slot

    def count_early(i, total):
        return total + (slot_of(i) < first).astype(jnp.int32)

    early = lax.fori_loop(0, blocks, count_early, jnp.int32(0))

    def copy(block, where):
        return pltpu.make_async_copy(data_ref.at[block], held_ref.at[where], sem.at[where])

    def place(i, at):
        low, high = at
        slot = slot_of(i)
        is_early = slot < first
        where = jnp.where(is_early, low, high)
        order_ref[where] = i
        slot_ref[where] = slot
        copy(i, where).start()
        one = is_early.astype(jnp.int32)
        return low + one, high + 1 - one

    lax.fori_loop(0, blocks, place, (jnp.int32(0), early))
    for where in range(blocks):
        copy(order_ref[where], where).wait()


def turn_sites(chips, width, slot, vector_ref, left_ref):
    here = lax.axis_index("space")
    chip, core = here // 2, here % 2
    real, imag = vector_ref[0], vector_ref[1]
    for part, pair in enumerate(((real, imag), (-imag, real))):
        turned = jnp.concatenate(pair, axis=0).T
        for to_chip in range(chips):
            for to_core in range(2):
                stays = (core == to_core).astype(jnp.int32)
                at = ((stays * chips + apart(chip, to_chip, chips)) * 2 + part) * width
                start = (to_chip * 2 + to_core) * width
                left_ref[slot, pl.ds(pl.multiple_of(at, width), width), :] = turned[
                    start : start + width
                ]


def project_sites(chips, width, start, slot_ref, left_ref, held_ref, give_refs, keep_ref):
    spins, columns = held_ref.shape[1], held_ref.shape[-1]
    rows = 2 * width
    for i in range(keep_ref.shape[1]):
        left = left_ref[slot_ref[start + i]]
        for spin in range(0, spins, 2):
            right = jnp.concatenate(
                [held_ref[start + i, s].reshape(-1, columns) for s in range(spin, spin + 2)],
                axis=1,
            )
            result = jnp.dot(left, right, preferred_element_type=jnp.float32)
            result = result.astype(keep_ref.dtype)
            for s in range(2):
                side = result[:, s * columns : (s + 1) * columns]
                parts = side.reshape(2, chips, rows, columns)
                give_refs[0][0, i, spin + s] = parts[0, 0]
                give_refs[1][:, i, spin + s] = parts[0, 1:]
                keep_ref[:, i, spin + s] = parts[1]


def project(chips, width, start, known, fresh, slot_ref, *refs):
    vector_refs, held_ref = refs[:fresh], refs[fresh]
    if fresh:
        *give_refs, keep_ref, left_ref = refs[-4:]
        for at, ref in enumerate(vector_refs):
            turn_sites(chips, width, known + at, ref, left_ref)
    else:
        left_ref = refs[1]
        *give_refs, keep_ref = refs[-3:]
    project_sites(chips, width, start, slot_ref, left_ref, held_ref, give_refs, keep_ref)


def finish(start, size, terms, order_ref, *refs):
    out_ref, stage_ref, sem = refs[-3:]

    def copy(i):
        return pltpu.make_async_copy(stage_ref.at[i], out_ref.at[order_ref[start + i]], sem.at[i])

    for i in range(size):
        total = None
        for ref in refs[:terms]:
            term = ref[i] if len(ref.shape) == 4 else ref[0, i]
            term = term.astype(jnp.float32)
            total = term if total is None else total + term
        stage_ref[i] = total.reshape(stage_ref.shape[1:]).astype(stage_ref.dtype)
        copy(i).start()
    for i in range(size):
        copy(i).wait()


def shards(solutions, eigvecs, sink_time):
    blocks, spins, _, colours, sites, columns = solutions.shape
    times = lax.axis_size("tm")
    members = lax.axis_size("space")
    chips = members // 2
    width = eigvecs.shape[-1] // members
    rows = 2 * width
    depth = 2 * colours * sites
    kind = solutions.dtype
    cores = [(i, i ^ 1) for i in range(members)]

    most = max(2, (2 * blocks + times - 1) // times)
    half = blocks // 2
    late = half // most
    first = times - late
    steps = [0] + list(range(1, times, 2)) + list(range(2, times, 2))

    own = eigvecs[0].reshape(2, colours * sites, -1)
    data = solutions.reshape(blocks, spins, 2, colours * sites, columns)
    vectors = [own]
    for slot, step in enumerate(steps[1:], 1):
        if slot >= first and in_pairs(times) and steps.index(step ^ 1) < first:
            vectors.append(swap(vectors[steps.index(step ^ 1)], "tm", 1, times))
        else:
            vectors.append(swap(own, "tm", step, times))

    numbers = pltpu.SMEM((blocks,), jnp.int32)
    order, slots, held = call(
        functools.partial(load, steps, first),
        [SMEM, HBM],
        [(SMEM, numbers), (SMEM, numbers), (VMEM, pltpu.VMEM(data.shape, kind))],
        [sink_time[:, 0], far(data)],
        scratch_shapes=[pltpu.SemaphoreType.DMA((blocks,))],
    )
    held = near(held)
    order, slots = scalars(order), scalars(slots)

    sizes = [share * blocks // 16 for share in SHARES]
    vectors = [near(v) for v in vectors]
    lefts = (VMEM, pltpu.VMEM((times, 4 * chips * width, depth), kind))
    left = None
    known = start = 0
    terms = []
    sents = []
    for at, size in enumerate(sizes):
        pieces = [
            (VMEM, pltpu.VMEM((count, size, spins, rows, columns), kind))
            for count in (1, chips - 1, chips)
        ]
        wanted = first if start + size <= half else times
        fresh = wanted - known
        after = sents[AFTER[at] : AFTER[at] + 1] if AFTER[at] is not None else []
        operands = [slots, *vectors[known:wanted], held]
        ins = [SMEM] + [VMEM] * (fresh + 1)
        if left is not None:
            operands.append(near(left))
            ins.append(VMEM)
        results = call(
            functools.partial(project, chips, width, start, known, fresh),
            ins + [ANY] * len(after),
            pieces + [lefts] * bool(fresh),
            operands + after,
            input_output_aliases={len(operands) - 1: 3} if fresh and left is not None else {},
        )
        give_near, give_far, keep = results[:3]
        if fresh:
            left = results[3]
        got = lax.ppermute(give_far, "space", cores)
        sums = [keep, lax.ppermute(give_near, "space", cores)]
        for step in range(1, chips):
            sent = (keep[step].astype(jnp.float32) + got[step - 1].astype(jnp.float32)).astype(kind)
            sums.append(send(sent, step, members))
        sents.append(sent)
        terms.append(sums)
        known = wanted
        start += size

    result = None
    start = 0
    for size, sums in zip(sizes, terms):
        operands = [order, *[near(a) for a in sums]]
        ins = [SMEM] + [VMEM] * len(sums)
        aliases = {}
        if result is not None:
            aliases = {len(operands): 0}
            operands.append(result)
            ins.append(HBM)
        (result,) = call(
            functools.partial(finish, start, size, len(sums)),
            ins,
            [(HBM, jax.ShapeDtypeStruct((blocks, spins, 2, width, columns), kind))],
            operands,
            MUCH,
            scratch_shapes=[
                pltpu.VMEM((size, spins, 2, width, columns), kind),
                pltpu.SemaphoreType.DMA((size,)),
            ],
            input_output_aliases=aliases,
        )
        start += size
    return result


def send(array, step, members):
    route = [(i, peer(i // 2, step, members // 2) * 2 + i % 2) for i in range(members)]
    return lax.ppermute(array, "space", route)


def solution(mesh):
    in_specs = (
        P(("grp", "tm"), None, None, None, "space", None),
        P("tm", None, None, "space", None),
        P(("grp", "tm"), None),
    )
    out_specs = P(("grp", "tm"), None, None, "space", None)
    return jax.shard_map(shards, mesh=mesh, in_specs=in_specs, out_specs=out_specs, check_vma=False)
```

```python
import functools

import jax
import jax.numpy as jnp
from jax import lax
from jax.experimental import pallas as pl
from jax.experimental.pallas import tpu as pltpu
from jax.sharding import PartitionSpec as P

SHARES = (4, 4, 8)
AFTER = (None, None, 1)
HOME_AFTER = 2
HOMES_BEFORE = 2
RELAY_AFTER = 0
SMEM = pl.BlockSpec(memory_space=pltpu.SMEM)
VMEM = pl.BlockSpec(memory_space=pltpu.VMEM)
HBM = pl.BlockSpec(memory_space=pltpu.HBM)
ANY = pl.BlockSpec(memory_space=pl.ANY)
LITTLE = pl.CostEstimate(flops=1, bytes_accessed=1, transcendentals=0)
MUCH = pl.CostEstimate(flops=20_000_000_000, bytes_accessed=1, transcendentals=0)
PARAMS = pltpu.CompilerParams(vmem_limit_bytes=16 * 1024 * 1024)


def near(array):
    return pltpu.with_memory_space_constraint(array, pltpu.VMEM)


def far(array):
    return pltpu.with_memory_space_constraint(array, pltpu.HBM)


def scalars(array):
    return pltpu.with_memory_space_constraint(array, pltpu.SMEM)


def in_pairs(count):
    return count & (count - 1) == 0


def peer(index, step, count):
    return index ^ step if in_pairs(count) else (index + step) % count


def apart(here, there, count):
    return here ^ there if in_pairs(count) else lax.rem(there - here + count, count)


def swap(array, axis, step, count):
    return lax.ppermute(array, axis, [(i, peer(i, step, count)) for i in range(count)])


def send(array, step, members):
    route = [(i, peer(i // 2, step, members // 2) * 2 + i % 2) for i in range(members)]
    return lax.ppermute(array, "space", route)


def call(kernel, ins, outs, operands, cost=LITTLE, **more):
    specs, shapes = zip(*outs)
    return pl.pallas_call(
        kernel,
        in_specs=ins,
        out_specs=specs,
        out_shape=shapes,
        cost_estimate=cost,
        compiler_params=PARAMS,
        **more,
    )(*operands)


def interleave(real, imag):
    whole = real.shape[0] // 128 * 128
    pieces = [real[:whole], imag[:whole], real[whole:], imag[whole:]]
    return jnp.concatenate([p for p in pieces if p.shape[0]], axis=0)


def quarter_turn(rows):
    whole = rows.shape[1] // 256 * 128
    edge = 2 * whole + (rows.shape[1] - 2 * whole) // 2
    pieces = [-rows[:, whole : 2 * whole], rows[:, :whole], -rows[:, edge:], rows[:, 2 * whole : edge]]
    return jnp.concatenate([p for p in pieces if p.shape[1]], axis=1)


def lay(chips, rows, source_ref, away_ref, home_ref, vector_ref, sem):
    copy = pltpu.make_async_copy(source_ref, vector_ref, sem)
    copy.start()
    copy.wait()
    turned = interleave(vector_ref[0], vector_ref[1]).T
    chip = lax.axis_index("space") // 2
    for to_chip in range(chips):
        part = turned[to_chip * rows : (to_chip + 1) * rows]
        step = apart(chip, to_chip, chips)

        @pl.when(step == 0)
        def _():
            home_ref[...] = part

        @pl.when(step > 0)
        def _():
            away_ref[jnp.maximum(step, 1) - 1] = part


def load(steps, first, source_ref, data_ref, order_ref, slot_ref, held_ref, times_ref, times_sem, sem):
    blocks = times_ref.shape[0]
    half = held_ref.shape[0]
    count = len(steps)
    here = lax.axis_index("tm")
    times = pltpu.make_async_copy(source_ref, times_ref, times_sem)
    times.start()
    times.wait()

    def copy(block, at):
        return pltpu.make_async_copy(data_ref.at[block], held_ref.at[at], sem.at[at])

    low, high = jnp.int32(0), jnp.int32(blocks - 1)
    for i in range(blocks):
        step = apart(times_ref[i], here, count)
        slot = jnp.int32(0)
        for at, value in enumerate(steps):
            slot = jnp.where(step == value, at, slot)
        early = slot < first
        where = jnp.where(early, low, high)
        order_ref[where] = i
        slot_ref[where] = slot
        pl.when(early & (low < half))(copy(i, jnp.minimum(low, half - 1)).start)
        one = early.astype(jnp.int32)
        low, high = low + one, high - 1 + one
    for at in range(half):
        copy(order_ref[at], at).wait()


def fill(width, rows, left_ref, slot, first_step, vector):
    core = lax.axis_index("space") % 2
    steps = left_ref.shape[1] // (2 * rows)
    for part, block in enumerate((vector, quarter_turn(vector))):
        for to_core in range(2):
            stays = (core == to_core).astype(jnp.int32)
            at = ((stays * steps + first_step) * 2 + part) * width
            left_ref[slot, pl.ds(pl.multiple_of(at, width), width), :] = block[
                to_core * width : (to_core + 1) * width
            ]


def multiply(left, block_ref, give_ref, keep_ref, i):
    spins, columns = block_ref.shape[0], block_ref.shape[-1]
    for spin in range(0, spins, 2):
        right = jnp.concatenate(
            [interleave(block_ref[s, 0], block_ref[s, 1]) for s in range(spin, spin + 2)], axis=1
        )
        result = jnp.dot(left, right, preferred_element_type=jnp.float32).astype(give_ref.dtype)
        for s in range(2):
            side = result[:, s * columns : (s + 1) * columns]
            parts = side.reshape(2, give_ref.shape[0], -1, columns)
            give_ref[:, i, spin + s] = parts[0]
            keep_ref[:, i, spin + s] = parts[1]


def project_away(width, rows, start, known, fresh, fetch, whole, order_ref, slot_ref, *refs):
    vector_refs, source_ref = refs[:fresh], refs[fresh]
    refs = list(refs)
    sem = refs.pop() if fetch else None
    whole_ref = refs.pop() if whole else None
    left_ref = refs.pop() if fresh else refs[fresh + 1]
    held_ref, base = (refs.pop(), 0) if fetch else (source_ref, start)
    give_ref, keep_ref = refs[-2:]
    size = give_ref.shape[1]

    def copy(i):
        return pltpu.make_async_copy(source_ref.at[order_ref[start + i]], held_ref.at[i], sem.at[i])

    if fetch:
        for i in range(size):
            copy(i).start()
    for slot, ref in enumerate(vector_refs):
        if known + slot == whole:
            chips = whole_ref.shape[0]
            chip = lax.axis_index("space") // 2
            turned = interleave(ref[0], ref[1]).T
            for to_chip in range(chips):
                whole_ref[apart(chip, to_chip, chips)] = turned[to_chip * rows : (to_chip + 1) * rows]
            ref = whole_ref.at[pl.ds(1, chips - 1)]
        for step in range(ref.shape[0]):
            fill(width, rows, left_ref, known + slot, step, ref[step])
    for i in range(size):
        if fetch:
            copy(i).wait()
        multiply(left_ref[slot_ref[start + i]], held_ref.at[base + i], give_ref, keep_ref, i)


def project_home(width, rows, slot_ref, *refs):
    give_ref, keep_ref, left_ref = refs[-3:]
    times = left_ref.shape[0]
    for slot, ref in enumerate(refs[:times]):
        fill(width, rows, left_ref, slot, 0, ref[0] if len(ref.shape) == 3 else ref[...])
    at = 0
    for held_ref in refs[times:-4]:
        for i in range(held_ref.shape[0]):
            multiply(left_ref[slot_ref[at]], held_ref.at[i], give_ref, keep_ref, at)
            at += 1


def mark(*refs):
    refs[-1][0] = 0


def relay(from_ref, _, to_ref):
    to_ref[...] = from_ref[...]


def finish(start, size, terms, order_ref, *refs):
    out_ref, stage_ref, sem = refs[-3:]

    def copy(i):
        return pltpu.make_async_copy(stage_ref.at[i], out_ref.at[order_ref[start + i]], sem.at[i])

    for i in range(size):
        total = None
        for ref in refs[:terms]:
            term = ref[i] if len(ref.shape) == 4 else ref[0, start + i]
            term = term.astype(jnp.float32)
            total = term if total is None else total + term
        stage_ref[i] = total.reshape(stage_ref.shape[1:]).astype(stage_ref.dtype)
        copy(i).start()
    for i in range(size):
        copy(i).wait()


def shards(solutions, eigvecs, sink_time):
    blocks, spins, _, colours, sites, columns = solutions.shape
    times = lax.axis_size("tm")
    members = lax.axis_size("space")
    chips = members // 2
    width = eigvecs.shape[-1] // members
    rows = 2 * width
    depth = 2 * colours * sites
    kind = solutions.dtype
    cores = [(i, i ^ 1) for i in range(members)]

    most = max(2, (2 * blocks + times - 1) // times)
    half = blocks // 2
    late = half // most
    first = times - late
    steps = [0] + list(range(1, times, 2)) + list(range(2, times, 2))

    own = eigvecs[0].reshape(2, colours * sites, -1)
    data = far(solutions.reshape(blocks, spins, 2, colours * sites, columns))
    away_kind = (VMEM, pltpu.VMEM((chips - 1, rows, depth), kind))
    all_kind = (VMEM, pltpu.VMEM((chips, rows, depth), kind))
    home_kind = (VMEM, pltpu.VMEM((rows, depth), kind))
    away, home = call(
        functools.partial(lay, chips, rows),
        [HBM],
        [away_kind, home_kind],
        [far(own)],
        scratch_shapes=[pltpu.VMEM(own.shape, kind), pltpu.SemaphoreType.DMA],
    )
    aways = [away] + [
        swap(own if step == steps[1] else away, "tm", step, times) for step in steps[1:first]
    ]

    sizes = [share * blocks // 16 for share in SHARES]
    numbers = (SMEM, pltpu.SMEM((blocks,), jnp.int32))

    def holding(size):
        return (VMEM, pltpu.VMEM((size, *data.shape[1:]), kind))

    def sums(count, size):
        return (VMEM, pltpu.VMEM((count, size, spins, rows, columns), kind))

    order, slots, held = call(
        functools.partial(load, steps, first),
        [HBM, HBM],
        [numbers, numbers, holding(half)],
        [far(sink_time[:, 0]), data],
        scratch_shapes=[
            pltpu.SMEM((blocks,), jnp.int32),
            pltpu.SemaphoreType.DMA,
            pltpu.SemaphoreType.DMA((half,)),
        ],
    )
    order, slots = scalars(order), scalars(slots)
    for step in steps[first:]:
        through = in_pairs(times) and steps.index(step ^ 1) < first
        aways.append(swap(aways[steps.index(step ^ 1)], "tm", 1, times) if through else swap(away, "tm", step, times))

    lefts = (VMEM, pltpu.VMEM((times, 2 * (chips - 1) * rows, depth), kind))
    left = None
    helds, sents, terms = [near(held)], [], []
    known = start = 0
    for at, size in enumerate(sizes):
        wanted = first if start + size <= half else times
        fresh = [near(a) for a in aways[known:wanted]]
        after = [] if AFTER[at] is None else [sents[AFTER[at]]]
        if at == HOMES_BEFORE:
            (home,) = call(relay, [VMEM, ANY], [home_kind], [near(home), sents[RELAY_AFTER]])
            homes = [home, nearest] + [swap(home, "tm", step, times) for step in steps[2:]]
        fetch = start >= half
        operands = [*fresh, data if fetch else helds[0]]
        ins = [VMEM] * len(fresh) + [HBM if fetch else VMEM]
        if left is not None:
            operands.append(near(left))
            ins.append(VMEM)
        outs = [sums(chips - 1, size)] * 2
        if fetch:
            outs.append(holding(size))
        if fresh:
            outs.append(lefts)
        whole = not start
        if whole:
            outs.append(all_kind)
        results = call(
            functools.partial(project_away, width, rows, start, known, len(fresh), fetch, int(whole)),
            [SMEM] * 2 + ins + [ANY] * len(after),
            outs,
            [order, slots, *operands, *after],
            scratch_shapes=[pltpu.SemaphoreType.DMA((size,))] if fetch else [],
            input_output_aliases={len(operands) + 1: len(outs) - 1} if fresh and left is not None else {},
        )
        give, keep = results[:2]
        if fetch:
            helds.append(near(results[2]))
        if fresh:
            left = results[2 + fetch]
        if whole:
            nearest = near(results[-1])
        got = lax.ppermute(give, "space", cores)
        arrived = []
        for step in range(1, chips):
            sent = keep[step - 1].astype(jnp.float32) + got[step - 1].astype(jnp.float32)
            sent = sent.astype(kind)
            arrived.append(send(sent, step, members))
        sents.append(sent)
        terms.append((start, size, arrived))
        known = wanted
        start += size

    give, keep = call(
        functools.partial(project_home, width, rows),
        [SMEM] + [VMEM] * (times + len(helds)) + [ANY],
        [sums(1, blocks)] * 2,
        [slots, *[near(h) for h in homes], *helds, sents[HOME_AFTER]],
        scratch_shapes=[pltpu.VMEM((times, 2 * rows, depth), kind)],
    )
    got = lax.ppermute(give, "space", cores)

    token = []
    for _, _, arrived in terms[:-1]:
        token = call(
            mark, [ANY] * (1 + len(token)), [(SMEM, pltpu.SMEM((1,), jnp.int32))], [arrived[-1], *token], MUCH
        )
    result = None
    for start, size, arrived in terms:
        arrays = [keep, got, *arrived]
        operands = [order, *[near(a) for a in arrays]]
        ins = [SMEM] + [VMEM] * len(arrays)
        aliases = {}
        if result is not None:
            aliases = {len(operands): 0}
            operands.append(result)
            ins.append(HBM)
        else:
            operands += token
            ins += [ANY] * len(token)
        (result,) = call(
            functools.partial(finish, start, size, len(arrays)),
            ins,
            [(HBM, jax.ShapeDtypeStruct((blocks, spins, 2, width, columns), kind))],
            operands,
            LITTLE,
            scratch_shapes=[
                pltpu.VMEM((size, spins, 2, width, columns), kind),
                pltpu.SemaphoreType.DMA((size,)),
            ],
            input_output_aliases=aliases,
        )
    return result


def solution(mesh):
    in_specs = (
        P(("grp", "tm"), None, None, None, "space", None),
        P("tm", None, None, "space", None),
        P(("grp", "tm"), None),
    )
    out_specs = P(("grp", "tm"), None, None, "space", None)
    return jax.shard_map(shards, mesh=mesh, in_specs=in_specs, out_specs=out_specs, check_vma=False)
```

```python
import functools

import jax
import jax.numpy as jnp
from jax import lax
from jax.experimental import pallas as pl
from jax.experimental.pallas import tpu as pltpu
from jax.sharding import PartitionSpec as P

SHARES = (3, 5, 8)
AFTER = (None, None, 1)
HOME_AFTER = 2
HOMES_BEFORE = 2
RELAY_AFTER = 1
SMEM = pl.BlockSpec(memory_space=pltpu.SMEM)
VMEM = pl.BlockSpec(memory_space=pltpu.VMEM)
HBM = pl.BlockSpec(memory_space=pltpu.HBM)
ANY = pl.BlockSpec(memory_space=pl.ANY)
LITTLE = pl.CostEstimate(flops=1, bytes_accessed=1, transcendentals=0)
MUCH = pl.CostEstimate(flops=20_000_000_000, bytes_accessed=1, transcendentals=0)
PARAMS = pltpu.CompilerParams(vmem_limit_bytes=16 * 1024 * 1024)


def near(array):
    return pltpu.with_memory_space_constraint(array, pltpu.VMEM)


def far(array):
    return pltpu.with_memory_space_constraint(array, pltpu.HBM)


def scalars(array):
    return pltpu.with_memory_space_constraint(array, pltpu.SMEM)


def in_pairs(count):
    return count & (count - 1) == 0


def peer(index, step, count):
    return index ^ step if in_pairs(count) else (index + step) % count


def apart(here, there, count):
    return here ^ there if in_pairs(count) else lax.rem(there - here + count, count)


def swap(array, axis, step, count):
    return lax.ppermute(array, axis, [(i, peer(i, step, count)) for i in range(count)])


def send(array, step, members):
    route = [(i, peer(i // 2, step, members // 2) * 2 + i % 2) for i in range(members)]
    return lax.ppermute(array, "space", route)


def call(kernel, ins, outs, operands, cost=LITTLE, **more):
    specs, shapes = zip(*outs)
    return pl.pallas_call(
        kernel,
        in_specs=ins,
        out_specs=specs,
        out_shape=shapes,
        cost_estimate=cost,
        compiler_params=PARAMS,
        **more,
    )(*operands)


def interleave(real, imag):
    whole = real.shape[0] // 128 * 128
    pieces = [real[:whole], imag[:whole], real[whole:], imag[whole:]]
    return jnp.concatenate([p for p in pieces if p.shape[0]], axis=0)


def quarter_turn(rows):
    whole = rows.shape[1] // 256 * 128
    edge = 2 * whole + (rows.shape[1] - 2 * whole) // 2
    pieces = [-rows[:, whole : 2 * whole], rows[:, :whole], -rows[:, edge:], rows[:, 2 * whole : edge]]
    return jnp.concatenate([p for p in pieces if p.shape[1]], axis=1)


def lay(chips, rows, source_ref, away_ref, home_ref, vector_ref, sem):
    cut = vector_ref.shape[1] // 2
    copies = [
        pltpu.make_async_copy(
            source_ref.at[part, pl.ds(at * cut, cut)],
            vector_ref.at[part, pl.ds(at * cut, cut)],
            sem.at[part, at],
        )
        for part in range(2)
        for at in range(2)
    ]
    for copy in copies:
        copy.start()
    for copy in copies:
        copy.wait()
    turned = interleave(vector_ref[0], vector_ref[1]).T
    chip = lax.axis_index("space") // 2
    for to_chip in range(chips):
        part = turned[to_chip * rows : (to_chip + 1) * rows]
        step = apart(chip, to_chip, chips)

        @pl.when(step == 0)
        def _():
            home_ref[...] = part

        @pl.when(step > 0)
        def _():
            away_ref[jnp.maximum(step, 1) - 1] = part


def load(steps, first, source_ref, data_ref, order_ref, slot_ref, held_ref, times_ref, times_sem, sem):
    blocks = times_ref.shape[0]
    half = held_ref.shape[0]
    count = len(steps)
    here = lax.axis_index("tm")
    times = pltpu.make_async_copy(source_ref, times_ref, times_sem)
    times.start()
    times.wait()

    def copy(block, at):
        return pltpu.make_async_copy(data_ref.at[block], held_ref.at[at], sem.at[at])

    low, high = jnp.int32(0), jnp.int32(blocks - 1)
    for i in range(blocks):
        step = apart(times_ref[i], here, count)
        slot = jnp.int32(0)
        for at, value in enumerate(steps):
            slot = jnp.where(step == value, at, slot)
        early = slot < first
        where = jnp.where(early, low, high)
        order_ref[where] = i
        slot_ref[where] = slot
        pl.when(early & (low < half))(copy(i, jnp.minimum(low, half - 1)).start)
        one = early.astype(jnp.int32)
        low, high = low + one, high - 1 + one
    for at in range(half):
        copy(order_ref[at], at).wait()


def fill(width, rows, left_ref, slot, first_step, vector):
    core = lax.axis_index("space") % 2
    steps = left_ref.shape[1] // (2 * rows)
    for part, block in enumerate((vector, quarter_turn(vector))):
        for to_core in range(2):
            stays = (core == to_core).astype(jnp.int32)
            at = ((stays * steps + first_step) * 2 + part) * width
            left_ref[slot, pl.ds(pl.multiple_of(at, width), width), :] = block[
                to_core * width : (to_core + 1) * width
            ]


def multiply(left, block_ref, give_ref, keep_ref, i):
    spins, columns = block_ref.shape[0], block_ref.shape[-1]
    for spin in range(0, spins, 2):
        right = jnp.concatenate(
            [interleave(block_ref[s, 0], block_ref[s, 1]) for s in range(spin, spin + 2)], axis=1
        )
        result = jnp.dot(left, right, preferred_element_type=jnp.float32).astype(give_ref.dtype)
        for s in range(2):
            side = result[:, s * columns : (s + 1) * columns]
            parts = side.reshape(2, give_ref.shape[0], -1, columns)
            give_ref[:, i, spin + s] = parts[0]
            keep_ref[:, i, spin + s] = parts[1]


def project_away(width, rows, start, known, fresh, fetch, whole, order_ref, slot_ref, *refs):
    vector_refs, source_ref = refs[:fresh], refs[fresh]
    refs = list(refs)
    sem = refs.pop() if fetch else None
    whole_ref = refs.pop() if whole else None
    left_ref = refs.pop() if fresh else refs[fresh + 1]
    held_ref, base = (refs.pop(), 0) if fetch else (source_ref, start)
    give_ref, keep_ref = refs[-2:]
    size = give_ref.shape[1]

    def copy(i):
        return pltpu.make_async_copy(source_ref.at[order_ref[start + i]], held_ref.at[i], sem.at[i])

    if fetch:
        for i in range(size):
            copy(i).start()
    for slot, ref in enumerate(vector_refs):
        if known + slot == whole:
            chips = whole_ref.shape[0]
            chip = lax.axis_index("space") // 2
            turned = interleave(ref[0], ref[1]).T
            for to_chip in range(chips):
                whole_ref[apart(chip, to_chip, chips)] = turned[to_chip * rows : (to_chip + 1) * rows]
            ref = whole_ref.at[pl.ds(1, chips - 1)]
        for step in range(ref.shape[0]):
            fill(width, rows, left_ref, known + slot, step, ref[step])
    for i in range(size):
        if fetch:
            copy(i).wait()
        multiply(left_ref[slot_ref[start + i]], held_ref.at[base + i], give_ref, keep_ref, i)


def project_home(width, rows, slot_ref, *refs):
    give_ref, keep_ref, left_ref = refs[-3:]
    times = left_ref.shape[0]
    for slot, ref in enumerate(refs[:times]):
        fill(width, rows, left_ref, slot, 0, ref[0] if len(ref.shape) == 3 else ref[...])
    at = 0
    for held_ref in refs[times:-4]:
        for i in range(held_ref.shape[0]):
            multiply(left_ref[slot_ref[at]], held_ref.at[i], give_ref, keep_ref, at)
            at += 1


def mark(*refs):
    refs[-1][0] = 0


def relay(from_ref, _, to_ref):
    to_ref[...] = from_ref[...]


def finish(start, size, terms, order_ref, *refs):
    out_ref, stage_ref, sem = refs[-3:]

    def copy(i):
        return pltpu.make_async_copy(stage_ref.at[i], out_ref.at[order_ref[start + i]], sem.at[i])

    for i in range(size):
        total = None
        for ref in refs[:terms]:
            term = ref[i] if len(ref.shape) == 4 else ref[0, start + i]
            term = term.astype(jnp.float32)
            total = term if total is None else total + term
        stage_ref[i] = total.reshape(stage_ref.shape[1:]).astype(stage_ref.dtype)
        copy(i).start()
    for i in range(size):
        copy(i).wait()


def shards(solutions, eigvecs, sink_time):
    blocks, spins, _, colours, sites, columns = solutions.shape
    times = lax.axis_size("tm")
    members = lax.axis_size("space")
    chips = members // 2
    width = eigvecs.shape[-1] // members
    rows = 2 * width
    depth = 2 * colours * sites
    kind = solutions.dtype
    cores = [(i, i ^ 1) for i in range(members)]

    most = max(2, (2 * blocks + times - 1) // times)
    half = blocks // 2
    late = half // most
    first = times - late
    steps = list(range(times))

    own = eigvecs[0].reshape(2, colours * sites, -1)
    data = far(solutions.reshape(blocks, spins, 2, colours * sites, columns))
    away_kind = (VMEM, pltpu.VMEM((chips - 1, rows, depth), kind))
    all_kind = (VMEM, pltpu.VMEM((chips, rows, depth), kind))
    home_kind = (VMEM, pltpu.VMEM((rows, depth), kind))
    away, home = call(
        functools.partial(lay, chips, rows),
        [HBM],
        [away_kind, home_kind],
        [far(own)],
        scratch_shapes=[pltpu.VMEM(own.shape, kind), pltpu.SemaphoreType.DMA((2, 2))],
    )
    aways = [away] + [
        swap(own if step == steps[1] else away, "tm", step, times) for step in steps[1:first]
    ]

    sizes = [share * blocks // 16 for share in SHARES]
    numbers = (SMEM, pltpu.SMEM((blocks,), jnp.int32))

    def holding(size):
        return (VMEM, pltpu.VMEM((size, *data.shape[1:]), kind))

    def sums(count, size):
        return (VMEM, pltpu.VMEM((count, size, spins, rows, columns), kind))

    order, slots, held = call(
        functools.partial(load, steps, first),
        [HBM, HBM],
        [numbers, numbers, holding(half)],
        [far(sink_time[:, 0]), data],
        scratch_shapes=[
            pltpu.SMEM((blocks,), jnp.int32),
            pltpu.SemaphoreType.DMA,
            pltpu.SemaphoreType.DMA((half,)),
        ],
    )
    order, slots = scalars(order), scalars(slots)
    for step in steps[first:]:
        through = in_pairs(times) and steps.index(step ^ 1) < first
        aways.append(swap(aways[steps.index(step ^ 1)], "tm", 1, times) if through else swap(away, "tm", step, times))

    lefts = (VMEM, pltpu.VMEM((times, 2 * (chips - 1) * rows, depth), kind))
    left = None
    helds, sents, terms = [near(held)], [], []
    known = start = 0
    for at, size in enumerate(sizes):
        wanted = first if start + size <= half else times
        fresh = [near(a) for a in aways[known:wanted]]
        after = [] if AFTER[at] is None else [sents[AFTER[at]]]
        if at == HOMES_BEFORE:
            (home,) = call(relay, [VMEM, ANY], [home_kind], [near(home), sents[RELAY_AFTER]])
            homes = [home, nearest] + [swap(home, "tm", step, times) for step in steps[2:]]
        fetch = start >= half
        operands = [*fresh, data if fetch else helds[0]]
        ins = [VMEM] * len(fresh) + [HBM if fetch else VMEM]
        if left is not None:
            operands.append(near(left))
            ins.append(VMEM)
        outs = [sums(chips - 1, size)] * 2
        if fetch:
            outs.append(holding(size))
        if fresh:
            outs.append(lefts)
        whole = not start
        if whole:
            outs.append(all_kind)
        results = call(
            functools.partial(project_away, width, rows, start, known, len(fresh), fetch, int(whole)),
            [SMEM] * 2 + ins + [ANY] * len(after),
            outs,
            [order, slots, *operands, *after],
            scratch_shapes=[pltpu.SemaphoreType.DMA((size,))] if fetch else [],
            input_output_aliases={len(operands) + 1: len(outs) - 1} if fresh and left is not None else {},
        )
        give, keep = results[:2]
        if fetch:
            helds.append(near(results[2]))
        if fresh:
            left = results[2 + fetch]
        if whole:
            nearest = near(results[-1])
        got = lax.ppermute(give, "space", cores)
        arrived = []
        for step in range(1, chips):
            sent = keep[step - 1].astype(jnp.float32) + got[step - 1].astype(jnp.float32)
            sent = sent.astype(kind)
            arrived.append(send(sent, step, members))
        sents.append(sent)
        terms.append((start, size, arrived))
        known = wanted
        start += size

    give, keep = call(
        functools.partial(project_home, width, rows),
        [SMEM] + [VMEM] * (times + len(helds)) + [ANY],
        [sums(1, blocks)] * 2,
        [slots, *[near(h) for h in homes], *helds, sents[HOME_AFTER]],
        scratch_shapes=[pltpu.VMEM((times, 2 * rows, depth), kind)],
    )
    got = lax.ppermute(give, "space", cores)

    token = []
    for _, _, arrived in terms[:-1]:
        token = call(
            mark, [ANY] * (1 + len(token)), [(SMEM, pltpu.SMEM((1,), jnp.int32))], [arrived[-1], *token], MUCH
        )
    result = None
    for start, size, arrived in terms:
        arrays = [keep, got, *arrived]
        operands = [order, *[near(a) for a in arrays]]
        ins = [SMEM] + [VMEM] * len(arrays)
        aliases = {}
        if result is not None:
            aliases = {len(operands): 0}
            operands.append(result)
            ins.append(HBM)
        else:
            operands += token
            ins += [ANY] * len(token)
        (result,) = call(
            functools.partial(finish, start, size, len(arrays)),
            ins,
            [(HBM, jax.ShapeDtypeStruct((blocks, spins, 2, width, columns), kind))],
            operands,
            LITTLE,
            scratch_shapes=[
                pltpu.VMEM((size, spins, 2, width, columns), kind),
                pltpu.SemaphoreType.DMA((size,)),
            ],
            input_output_aliases=aliases,
        )
    return result


def solution(mesh):
    in_specs = (
        P(("grp", "tm"), None, None, None, "space", None),
        P("tm", None, None, "space", None),
        P(("grp", "tm"), None),
    )
    out_specs = P(("grp", "tm"), None, None, "space", None)
    return jax.shard_map(shards, mesh=mesh, in_specs=in_specs, out_specs=out_specs, check_vma=False)
```

```python
import functools

import jax
import jax.numpy as jnp
from jax import lax
from jax.experimental import pallas as pl
from jax.experimental.pallas import tpu as pltpu
from jax.sharding import PartitionSpec as P

SHARES = (2, 6, 8)
AFTER = (None, None, 1)
HOME_AFTER = 2
HOMES_BEFORE = 2
RELAY_AFTER = 1
SMEM = pl.BlockSpec(memory_space=pltpu.SMEM)
VMEM = pl.BlockSpec(memory_space=pltpu.VMEM)
HBM = pl.BlockSpec(memory_space=pltpu.HBM)
ANY = pl.BlockSpec(memory_space=pl.ANY)
LITTLE = pl.CostEstimate(flops=1, bytes_accessed=1, transcendentals=0)
MUCH = pl.CostEstimate(flops=20_000_000_000, bytes_accessed=1, transcendentals=0)
PARAMS = pltpu.CompilerParams(vmem_limit_bytes=16 * 1024 * 1024)


def near(array):
    return pltpu.with_memory_space_constraint(array, pltpu.VMEM)


def far(array):
    return pltpu.with_memory_space_constraint(array, pltpu.HBM)


def scalars(array):
    return pltpu.with_memory_space_constraint(array, pltpu.SMEM)


def in_pairs(count):
    return count & (count - 1) == 0


def peer(index, step, count):
    return index ^ step if in_pairs(count) else (index + step) % count


def apart(here, there, count):
    return here ^ there if in_pairs(count) else lax.rem(there - here + count, count)


def swap(array, axis, step, count):
    return lax.ppermute(array, axis, [(i, peer(i, step, count)) for i in range(count)])


def send(array, step, members):
    route = [(i, peer(i // 2, step, members // 2) * 2 + i % 2) for i in range(members)]
    return lax.ppermute(array, "space", route)


def call(kernel, ins, outs, operands, cost=LITTLE, **more):
    specs, shapes = zip(*outs)
    return pl.pallas_call(
        kernel,
        in_specs=ins,
        out_specs=specs,
        out_shape=shapes,
        cost_estimate=cost,
        compiler_params=PARAMS,
        **more,
    )(*operands)


def interleave(real, imag):
    whole = real.shape[0] // 128 * 128
    pieces = [real[:whole], imag[:whole], real[whole:], imag[whole:]]
    return jnp.concatenate([p for p in pieces if p.shape[0]], axis=0)


def quarter_turn(rows):
    whole = rows.shape[1] // 256 * 128
    edge = 2 * whole + (rows.shape[1] - 2 * whole) // 2
    pieces = [-rows[:, whole : 2 * whole], rows[:, :whole], -rows[:, edge:], rows[:, 2 * whole : edge]]
    return jnp.concatenate([p for p in pieces if p.shape[1]], axis=1)


def lay(chips, rows, source_ref, away_ref, home_ref, vector_ref, sem):
    cut = vector_ref.shape[1] // 2
    copies = [
        pltpu.make_async_copy(
            source_ref.at[part, pl.ds(at * cut, cut)],
            vector_ref.at[part, pl.ds(at * cut, cut)],
            sem.at[part, at],
        )
        for part in range(2)
        for at in range(2)
    ]
    for copy in copies:
        copy.start()
    for copy in copies:
        copy.wait()
    turned = interleave(vector_ref[0], vector_ref[1]).T
    chip = lax.axis_index("space") // 2
    for to_chip in range(chips):
        part = turned[to_chip * rows : (to_chip + 1) * rows]
        step = apart(chip, to_chip, chips)

        @pl.when(step == 0)
        def _():
            home_ref[...] = part

        @pl.when(step > 0)
        def _():
            away_ref[jnp.maximum(step, 1) - 1] = part


def load(steps, first, source_ref, data_ref, order_ref, slot_ref, held_ref, times_ref, times_sem, sem):
    blocks = times_ref.shape[0]
    half = held_ref.shape[0]
    count = len(steps)
    here = lax.axis_index("tm")
    times = pltpu.make_async_copy(source_ref, times_ref, times_sem)
    times.start()
    times.wait()

    def copy(block, at):
        return pltpu.make_async_copy(data_ref.at[block], held_ref.at[at], sem.at[at])

    low, high = jnp.int32(0), jnp.int32(blocks - 1)
    for i in range(blocks):
        step = apart(times_ref[i], here, count)
        slot = jnp.int32(0)
        for at, value in enumerate(steps):
            slot = jnp.where(step == value, at, slot)
        early = slot < first
        where = jnp.where(early, low, high)
        order_ref[where] = i
        slot_ref[where] = slot
        pl.when(early & (low < half))(copy(i, jnp.minimum(low, half - 1)).start)
        one = early.astype(jnp.int32)
        low, high = low + one, high - 1 + one
    for at in range(half):
        copy(order_ref[at], at).wait()


def fill(width, rows, left_ref, slot, first_step, vector):
    core = lax.axis_index("space") % 2
    steps = left_ref.shape[1] // (2 * rows)
    for part, block in enumerate((vector, quarter_turn(vector))):
        for to_core in range(2):
            stays = (core == to_core).astype(jnp.int32)
            at = ((stays * steps + first_step) * 2 + part) * width
            left_ref[slot, pl.ds(pl.multiple_of(at, width), width), :] = block[
                to_core * width : (to_core + 1) * width
            ]


def multiply(left, block_ref, give_ref, keep_ref, i):
    spins, columns = block_ref.shape[0], block_ref.shape[-1]
    for spin in range(0, spins, 2):
        right = jnp.concatenate(
            [interleave(block_ref[s, 0], block_ref[s, 1]) for s in range(spin, spin + 2)], axis=1
        )
        result = jnp.dot(left, right, preferred_element_type=jnp.float32).astype(give_ref.dtype)
        for s in range(2):
            side = result[:, s * columns : (s + 1) * columns]
            parts = side.reshape(2, give_ref.shape[0], -1, columns)
            give_ref[:, i, spin + s] = parts[0]
            keep_ref[:, i, spin + s] = parts[1]


def project_away(width, rows, start, known, fresh, fetch, whole, order_ref, slot_ref, *refs):
    vector_refs, source_ref = refs[:fresh], refs[fresh]
    refs = list(refs)
    sem = refs.pop() if fetch else None
    whole_ref = refs.pop() if whole else None
    left_ref = refs.pop() if fresh else refs[fresh + 1]
    held_ref, base = (refs.pop(), 0) if fetch else (source_ref, start)
    give_ref, keep_ref = refs[-2:]
    size = give_ref.shape[1]

    def copy(i):
        return pltpu.make_async_copy(source_ref.at[order_ref[start + i]], held_ref.at[i], sem.at[i])

    if fetch:
        for i in range(size):
            copy(i).start()
    for slot, ref in enumerate(vector_refs):
        if known + slot == whole:
            chips = whole_ref.shape[0]
            chip = lax.axis_index("space") // 2
            turned = interleave(ref[0], ref[1]).T
            for to_chip in range(chips):
                whole_ref[apart(chip, to_chip, chips)] = turned[to_chip * rows : (to_chip + 1) * rows]
            ref = whole_ref.at[pl.ds(1, chips - 1)]
        for step in range(ref.shape[0]):
            fill(width, rows, left_ref, known + slot, step, ref[step])
    for i in range(size):
        if fetch:
            copy(i).wait()
        multiply(left_ref[slot_ref[start + i]], held_ref.at[base + i], give_ref, keep_ref, i)


def project_home(width, rows, slot_ref, *refs):
    give_ref, keep_ref, left_ref = refs[-3:]
    times = left_ref.shape[0]
    for slot, ref in enumerate(refs[:times]):
        fill(width, rows, left_ref, slot, 0, ref[0] if len(ref.shape) == 3 else ref[...])
    at = 0
    for held_ref in refs[times:-4]:
        for i in range(held_ref.shape[0]):
            multiply(left_ref[slot_ref[at]], held_ref.at[i], give_ref, keep_ref, at)
            at += 1


def mark(*refs):
    refs[-1][0] = 0


def relay(from_ref, _, to_ref):
    to_ref[...] = from_ref[...]


def finish(start, size, terms, order_ref, *refs):
    out_ref, stage_ref, sem = refs[-3:]

    def copy(i):
        return pltpu.make_async_copy(stage_ref.at[i], out_ref.at[order_ref[start + i]], sem.at[i])

    for i in range(size):
        total = None
        for ref in refs[:terms]:
            term = ref[i] if len(ref.shape) == 4 else ref[0, start + i]
            term = term.astype(jnp.float32)
            total = term if total is None else total + term
        stage_ref[i] = total.reshape(stage_ref.shape[1:]).astype(stage_ref.dtype)
        copy(i).start()
    for i in range(size):
        copy(i).wait()


def shards(solutions, eigvecs, sink_time):
    blocks, spins, _, colours, sites, columns = solutions.shape
    times = lax.axis_size("tm")
    members = lax.axis_size("space")
    chips = members // 2
    width = eigvecs.shape[-1] // members
    rows = 2 * width
    depth = 2 * colours * sites
    kind = solutions.dtype
    cores = [(i, i ^ 1) for i in range(members)]

    most = max(2, (2 * blocks + times - 1) // times)
    half = blocks // 2
    late = half // most
    first = times - late
    steps = list(range(times))

    own = eigvecs[0].reshape(2, colours * sites, -1)
    data = far(solutions.reshape(blocks, spins, 2, colours * sites, columns))
    away_kind = (VMEM, pltpu.VMEM((chips - 1, rows, depth), kind))
    all_kind = (VMEM, pltpu.VMEM((chips, rows, depth), kind))
    home_kind = (VMEM, pltpu.VMEM((rows, depth), kind))
    away, home = call(
        functools.partial(lay, chips, rows),
        [HBM],
        [away_kind, home_kind],
        [far(own)],
        scratch_shapes=[pltpu.VMEM(own.shape, kind), pltpu.SemaphoreType.DMA((2, 2))],
    )
    aways = [away] + [
        swap(own if step == steps[1] else away, "tm", step, times) for step in steps[1:first]
    ]

    sizes = [share * blocks // 16 for share in SHARES]
    numbers = (SMEM, pltpu.SMEM((blocks,), jnp.int32))

    def holding(size):
        return (VMEM, pltpu.VMEM((size, *data.shape[1:]), kind))

    def sums(count, size):
        return (VMEM, pltpu.VMEM((count, size, spins, rows, columns), kind))

    order, slots, held = call(
        functools.partial(load, steps, first),
        [HBM, HBM],
        [numbers, numbers, holding(half)],
        [far(sink_time[:, 0]), data],
        scratch_shapes=[
            pltpu.SMEM((blocks,), jnp.int32),
            pltpu.SemaphoreType.DMA,
            pltpu.SemaphoreType.DMA((half,)),
        ],
    )
    order, slots = scalars(order), scalars(slots)
    for step in steps[first:]:
        through = in_pairs(times) and steps.index(step ^ 1) < first
        aways.append(swap(aways[steps.index(step ^ 1)], "tm", 1, times) if through else swap(away, "tm", step, times))

    lefts = (VMEM, pltpu.VMEM((times, 2 * (chips - 1) * rows, depth), kind))
    left = None
    helds, sents, terms = [near(held)], [], []
    known = start = 0
    for at, size in enumerate(sizes):
        wanted = first if start + size <= half else times
        fresh = [near(a) for a in aways[known:wanted]]
        after = [] if AFTER[at] is None else [sents[AFTER[at]]]
        if at == HOMES_BEFORE:
            (home,) = call(relay, [VMEM, ANY], [home_kind], [near(home), sents[RELAY_AFTER]])
            homes = [home, nearest] + [swap(home, "tm", step, times) for step in steps[2:]]
        fetch = start >= half
        operands = [*fresh, data if fetch else helds[0]]
        ins = [VMEM] * len(fresh) + [HBM if fetch else VMEM]
        if left is not None:
            operands.append(near(left))
            ins.append(VMEM)
        outs = [sums(chips - 1, size)] * 2
        if fetch:
            outs.append(holding(size))
        if fresh:
            outs.append(lefts)
        whole = not start
        if whole:
            outs.append(all_kind)
        results = call(
            functools.partial(project_away, width, rows, start, known, len(fresh), fetch, int(whole)),
            [SMEM] * 2 + ins + [ANY] * len(after),
            outs,
            [order, slots, *operands, *after],
            scratch_shapes=[pltpu.SemaphoreType.DMA((size,))] if fetch else [],
            input_output_aliases={len(operands) + 1: len(outs) - 1} if fresh and left is not None else {},
        )
        give, keep = results[:2]
        if fetch:
            helds.append(near(results[2]))
        if fresh:
            left = results[2 + fetch]
        if whole:
            nearest = near(results[-1])
        got = lax.ppermute(give, "space", cores)
        arrived = []
        for step in range(1, chips):
            sent = keep[step - 1].astype(jnp.float32) + got[step - 1].astype(jnp.float32)
            sent = sent.astype(kind)
            arrived.append(send(sent, step, members))
        sents.append(sent)
        terms.append((start, size, arrived))
        known = wanted
        start += size

    give, keep = call(
        functools.partial(project_home, width, rows),
        [SMEM] + [VMEM] * (times + len(helds)) + [ANY],
        [sums(1, blocks)] * 2,
        [slots, *[near(h) for h in homes], *helds, sents[HOME_AFTER]],
        scratch_shapes=[pltpu.VMEM((times, 2 * rows, depth), kind)],
    )
    got = lax.ppermute(give, "space", cores)

    token = []
    for _, _, arrived in terms[:-1]:
        token = call(
            mark, [ANY] * (1 + len(token)), [(SMEM, pltpu.SMEM((1,), jnp.int32))], [arrived[-1], *token], MUCH
        )
    result = None
    for start, size, arrived in terms:
        arrays = [keep, got, *arrived]
        operands = [order, *[near(a) for a in arrays]]
        ins = [SMEM] + [VMEM] * len(arrays)
        aliases = {}
        if result is not None:
            aliases = {len(operands): 0}
            operands.append(result)
            ins.append(HBM)
        else:
            operands += token
            ins += [ANY] * len(token)
        (result,) = call(
            functools.partial(finish, start, size, len(arrays)),
            ins,
            [(HBM, jax.ShapeDtypeStruct((blocks, spins, 2, width, columns), kind))],
            operands,
            LITTLE,
            scratch_shapes=[
                pltpu.VMEM((size, spins, 2, width, columns), kind),
                pltpu.SemaphoreType.DMA((size,)),
            ],
            input_output_aliases=aliases,
        )
    return result


def solution(mesh):
    in_specs = (
        P(("grp", "tm"), None, None, None, "space", None),
        P("tm", None, None, "space", None),
        P(("grp", "tm"), None),
    )
    out_specs = P(("grp", "tm"), None, None, "space", None)
    return jax.shard_map(shards, mesh=mesh, in_specs=in_specs, out_specs=out_specs, check_vma=False)
```
